512 devices in a mesh: group: 16 (over z_lo, core), blk: 32 (over x, y, z_hi).
Axes of the slice: x: 4, y: 4, z: 16 (z_hi: 2, z_lo: 8; z = z_hi * 8 + z_lo), core: 2. Of those that a mesh axis runs over, the one named last changes fastest.
Arguments:
- image_emb: bfloat16 [262144, 1152], P(('group', 'blk')), may hold values from -0.1875 to 0.1875
- text_emb: bfloat16 [262144, 1152], P(('group', 'blk')), may hold values from -0.1875 to 0.1875
- labels: int32 [262144], P(('group', 'blk')), may hold values from 0 to 511, as said below
- log_scale: float32 [1], replicated, may hold values from 1 to 2
- bias: float32 [1], replicated, may hold values from -1.5 to -0.5
Outputs:
- grad_image: bfloat16 [262144, 1152], P(('group', 'blk'))
- grad_text: bfloat16 [262144, 1152], P(('group', 'blk'))
The draws below stay inside these ranges and needn't reach their ends.
Inputs may be any that keep to these rules, and one draw needn't show every extreme that they name: `labels`: within each aligned block of 512 rows the entries are a permutation of 0 to 511.
All inputs are finite; a program needn't handle non-finite values.
Results may differ from the reference program's by a relative error of at most 0.0064.
Values may be sent and summed in bfloat16 or wider, within the bound.
A program may use at most 64 MiB of HBM per device.

```python
import jax
import jax.numpy as jnp
from jax import lax

D = 1152
ROWS = 512
BLOCKS = 512
TOTAL = 262144
N_GROUP = 16
N_BLK = 32


def draw_labels(key, part):
    key = jax.random.fold_in(key, 7)
    keys = jax.random.split(key, BLOCKS)
    perms = jax.vmap(lambda k: jax.random.permutation(k, ROWS))(keys)
    return perms.reshape(-1).astype(jnp.int32)


def block_levels(stream_key, dims, pieces, smallest, largest):
    level, own = 1.0, jax.random.fold_in(stream_key, 6)
    for axis_at, shards_of in pieces:
        steps = jnp.exp(jax.random.uniform(jax.random.fold_in(own, axis_at), (shards_of,), jnp.float32, smallest / len(pieces), largest / len(pieces)))
        level = level * jnp.repeat(steps, dims[axis_at] // shards_of).reshape([-1 if axis == axis_at else 1 for axis in range(len(dims))])
    return level


def bell_draw(stream_key, shape, deviation, limit, shards=(), kind=jnp.bfloat16):
    drawn = deviation * jax.random.normal(stream_key, shape, jnp.float32)
    if shards:
        drawn = drawn * block_levels(stream_key, shape, shards, -0.22, 0.18)
    return jnp.clip(drawn, -limit, limit).astype(kind)


def setup_inputs(seed: int = 0) -> dict:
    seeds = jax.random.split(jax.random.key(seed), 6)
    image_emb = bell_draw(seeds[0], (TOTAL, D), D ** -0.5, 0.1875, ((0, 512),))
    text_emb = bell_draw(seeds[1], (TOTAL, D), D ** -0.5, 0.1875, ((0, 512),))
    labels = draw_labels(jax.random.fold_in(seeds[5], 71), 0)
    log_scale = jnp.clip(jax.random.uniform(seeds[3], (1,), jnp.float32, 1.0, 2.0), 1.0, 2.0)
    bias = jnp.clip(jax.random.uniform(seeds[4], (1,), jnp.float32, -1.5, -0.5), -1.5, -0.5)
    return {"image_emb": image_emb, "text_emb": text_emb, "labels": labels, "log_scale": log_scale, "bias": bias}


EPS = 1e-06

def unit_rows(v):
    f = v.astype(jnp.float32)
    inv = lax.rsqrt(lax.optimization_barrier(jnp.sum(f * f, axis=-1, keepdims=True)) + EPS)
    return (f * inv, inv)

def tile_terms(xh, yh, scale, shift_b, label):
    xf = xh.astype(jnp.float32)
    yf = yh.astype(jnp.float32)
    s = scale * jnp.einsum('bid,bjd->bij', xf, yf) + shift_b
    q = (jax.nn.sigmoid(s) - label).astype(jnp.bfloat16).astype(jnp.float32)
    dx = scale * jnp.einsum('bij,bjd->bid', q, yf)
    dy = scale * jnp.einsum('bij,bid->bjd', q, xf)
    return (dx, dy)

def rounded(term):
    return lax.optimization_barrier(term.astype(jnp.bfloat16)).astype(jnp.float32)

def reference(image_emb, text_emb, labels, log_scale, bias):
    scale = jnp.exp(log_scale[0])
    shift_b = bias[0]
    ximg, xinv = unit_rows(image_emb)
    ytxt, yinv = unit_rows(text_emb)
    xh = ximg.astype(jnp.bfloat16).reshape(N_GROUP, N_BLK, ROWS, D)
    yh = ytxt.astype(jnp.bfloat16).reshape(N_GROUP, N_BLK, ROWS, D)
    lab = labels.reshape(N_GROUP, N_BLK, ROWS)
    columns = jnp.arange(ROWS, dtype=jnp.int32)

    def one_group(g):
        g = g.astype(jnp.int32)
        x_own = lax.dynamic_index_in_dim(xh, g, 0, keepdims=False)
        x_next = lax.dynamic_index_in_dim(xh, (g + 1) % N_GROUP, 0, keepdims=False)
        y_own = lax.dynamic_index_in_dim(yh, g, 0, keepdims=False)
        y_prev = lax.dynamic_index_in_dim(yh, (g - 1 + N_GROUP) % N_GROUP, 0, keepdims=False)
        lab_g = lax.dynamic_index_in_dim(lab, g, 0, keepdims=False)
        onehot = (lab_g[:, :, None] == columns[None, None, :]).astype(jnp.float32)
        dx0, dy0 = tile_terms(x_own, y_own, scale, shift_b, onehot)
        dx1, _ = tile_terms(x_own, jnp.roll(y_own, 1, axis=0), scale, shift_b, 0.0)
        dx2, _ = tile_terms(x_own, y_prev, scale, shift_b, 0.0)
        _, dy1 = tile_terms(jnp.roll(x_own, -1, axis=0), y_own, scale, shift_b, 0.0)
        _, dy2 = tile_terms(x_next, y_own, scale, shift_b, 0.0)
        return (dx0 + dx1 + dx2, dy0 + rounded(dy1) + rounded(dy2))
    dxs, dys = lax.map(one_group, jnp.arange(N_GROUP, dtype=jnp.int32))
    dxh = dxs.reshape(TOTAL, D)
    dyh = dys.reshape(TOTAL, D)
    grad_image = ((dxh - ximg * lax.optimization_barrier(jnp.sum(ximg * dxh, axis=-1, keepdims=True))) * xinv).astype(jnp.bfloat16)
    grad_text = ((dyh - ytxt * lax.optimization_barrier(jnp.sum(ytxt * dyh, axis=-1, keepdims=True))) * yinv).astype(jnp.bfloat16)
    return (grad_image, grad_text)
```

```python
import functools

import jax
import jax.numpy as jnp
from jax import lax
from jax.experimental import pallas as pl
from jax.experimental.pallas import tpu as pltpu
from jax.sharding import PartitionSpec as P

EPS = 1e-06
MESH = pl.DeviceIdType.MESH
TEXT, IMAGE = 0, 1
HOPS = 8
WAVES = 2
CHUNKS = 4
GROUP_SLOT, LAST_SLOT = 7, 8
BAND = 128


def dot_nt(a, b):
    return lax.dot_general(a, b, (((1,), (1,)), ((), ())), preferred_element_type=jnp.float32)


def dot_tn(a, b):
    return lax.dot_general(a, b, (((0,), (0,)), ((), ())), preferred_element_type=jnp.float32)


def unit_rows(v):
    f = v.astype(jnp.float32)
    inv = lax.rsqrt(jnp.sum(f * f, axis=-1, keepdims=True) + EPS)
    return f * inv, inv


def kernel(
    rows, compute, scale_ref, bias_ref, label_ref, image_ref, text_ref, gimage_ref, gtext_ref,
    raw, unit, acc, piece_unit, stage, buf, load_sem, send_sem, recv_sem, side_sem, store_sem,
):
    g, b = lax.axis_index("group"), lax.axis_index("blk")
    core, z_lo = lax.rem(g, 2), lax.div(g, 2)
    z_hi, xy = lax.rem(b, 2), lax.div(b, 2)
    z = z_hi * 8 + z_lo
    other = 1 - core

    def device(z_to, core_to, xy_to):
        z_in = lax.rem(z_to + 32, 16)
        return lax.rem(z_in, 8) * 2 + core_to, lax.rem(xy_to + 16, 16) * 2 + lax.div(z_in, 8)

    def way(c):
        return 2 * c - 1

    def lane_core(lane, z_at, c):
        edge = 7 if lane == TEXT else 0
        return jnp.where(lax.rem(z_at + 32, 8) == edge, 1 - c, c)

    step = way(core)
    following, before = device(z + step, core, xy), device(z - step, core, xy)
    partner = device(z, other, xy)
    first, first_from, last, last_from = [], [], [], []
    for lane in (TEXT, IMAGE):
        own_lane = lane_core(lane, z, core)
        first.append(device(z + way(own_lane), own_lane, xy))
        first_from.append(device(z - step, lane_core(lane, z - step, core), xy))
        crossing = 0 if lane == TEXT else 1
        shift = 1 if lane == TEXT else -1
        last_hi = lax.div(lax.rem(z + step + 32, 16), 8)
        last.append(
            device(z + step, lane_core(lane, z + step, core), xy + jnp.where(last_hi == crossing, shift, 0))
        )
        last_from.append(
            device(z - way(own_lane), own_lane, xy - jnp.where(z_hi == crossing, shift, 0))
        )

    own = (text_ref, image_ref)
    part = rows // (WAVES * CHUNKS)
    wave_rows = rows // WAVES

    loads = [pltpu.make_async_copy(own[l], raw.at[l], load_sem.at[l]) for l in (TEXT, IMAGE)]
    for load in loads:
        load.start()

    barrier = pltpu.get_barrier_semaphore()
    for source in (before, partner, *first_from, *last_from):
        pl.semaphore_signal(barrier, inc=1, device_id=source, device_id_type=MESH)
    pl.semaphore_wait(barrier, 6)

    def chunk_rows(chunk):
        return pl.ds(pl.multiple_of(chunk * part, part), part)

    def hop(lane, src, slot, hop_at, chunk, to):
        at = chunk_rows(chunk)
        return pltpu.make_async_remote_copy(
            src_ref=src.at[at], dst_ref=buf.at[lane, slot, at], send_sem=send_sem.at[lane, hop_at],
            recv_sem=recv_sem.at[lane, slot, chunk], device_id=to, device_id_type=MESH,
        )

    def arrived(lane, slot, chunk):
        hop(lane, buf.at[lane, slot], slot, 0, chunk, following).wait_recv()

    own_side = core
    lane_side = other
    gives = jnp.where(core == 0, z_lo != 7, z_lo != 0)
    takes_lane = jnp.where(core == 0, z_lo == 0, z_lo == 7)

    def side(src, lane, kind, chunk):
        at = chunk_rows(chunk)
        return pltpu.make_async_remote_copy(
            src_ref=src.at[at], dst_ref=buf.at[lane, GROUP_SLOT, at], send_sem=side_sem.at[kind],
            recv_sem=recv_sem.at[lane, GROUP_SLOT, chunk], device_id=partner, device_id_type=MESH,
        )

    def first_round(w):
        for lane in (TEXT, IMAGE):
            @pl.loop(0, CHUNKS)
            def _(c):
                hop(lane, own[lane], 0, 0, w * CHUNKS + c, first[lane]).start()

        for lane in (TEXT, IMAGE):
            @pl.when(own_side == lane)
            def _():
                @pl.loop(0, CHUNKS)
                def _(c):
                    side(own[lane], lane, 0, w * CHUNKS + c).start()

    def relay_round(w, h):
        for lane in (TEXT, IMAGE):
            @pl.loop(0, CHUNKS)
            def _(c):
                chunk = w * CHUNKS + c
                arrived(lane, h - 1, chunk)
                hop(lane, buf.at[lane, h - 1], h, h, chunk, following).start()

                @pl.when((h == 1) & gives & (lane_side == lane))
                def _():
                    side(buf.at[lane, 0], lane, 1, chunk).start()

    def last_round(w):
        for lane in (TEXT, IMAGE):
            @pl.loop(0, CHUNKS)
            def _(c):
                chunk = w * CHUNKS + c
                arrived(lane, HOPS - 2, chunk)
                hop(lane, buf.at[lane, HOPS - 2], LAST_SLOT, HOPS - 1, chunk, last[lane]).start()

    scale = jnp.exp(jnp.full((1, 1), scale_ref[0], jnp.float32))
    shift_b = bias_ref[0]

    def prepare():
        for l in (TEXT, IMAGE):
            loads[l].wait()

            @pl.loop(0, rows // BAND)
            def _(i):
                at = pl.ds(pl.multiple_of(i * BAND, BAND), BAND)
                unit[l, at] = unit_rows(raw[l, at])[0].astype(jnp.bfloat16)

    def own_tile():
        acc[TEXT] = jnp.zeros_like(acc[TEXT])

        @pl.loop(0, rows // BAND)
        def _(i):
            at = pl.ds(pl.multiple_of(i * BAND, BAND), BAND)
            s = scale * dot_nt(unit[TEXT, at], unit[IMAGE]) + shift_b
            text_row = lax.broadcasted_iota(jnp.int32, s.shape, 0) + i * BAND
            label = (text_row == label_ref[...]).astype(jnp.float32)
            q = (jax.nn.sigmoid(s) - label).astype(jnp.bfloat16)
            acc[IMAGE, at] = jnp.dot(q, unit[IMAGE], preferred_element_type=jnp.float32)
            acc[TEXT] += dot_tn(q, unit[TEXT, at])

    def piece(lane, slot, start, count):
        piece_unit[0:count] = unit_rows(buf[lane, slot, pl.ds(start, count)])[0].astype(jnp.bfloat16)

        @pl.loop(0, rows // BAND)
        def _(i):
            at = pl.ds(pl.multiple_of(i * BAND, BAND), BAND)
            s = scale * dot_nt(unit[1 - lane, at], piece_unit[0:count]) + shift_b
            q = jax.nn.sigmoid(s).astype(jnp.bfloat16)
            acc[lane, at] += jnp.dot(q, piece_unit[0:count], preferred_element_type=jnp.float32)

    def group_pieces(w):
        slot = jnp.where(takes_lane, HOPS - 2, GROUP_SLOT)
        for lane in (TEXT, IMAGE):
            from_lane = takes_lane & (core == lane)

            @pl.when(jnp.logical_not(from_lane))
            def _():
                @pl.loop(0, CHUNKS)
                def _(c):
                    arrived(lane, GROUP_SLOT, w * CHUNKS + c)

            if compute:
                piece(lane, jnp.where(from_lane, HOPS - 2, GROUP_SLOT), w * wave_rows, wave_rows)

    def last_pieces(w):
        for lane in (TEXT, IMAGE):
            @pl.loop(0, CHUNKS)
            def _(c):
                arrived(lane, LAST_SLOT, w * CHUNKS + c)

            if compute:
                piece(lane, LAST_SLOT, w * wave_rows, wave_rows)

    def store(lane):
        out = (gimage_ref, gtext_ref)[lane]
        return pltpu.make_async_copy(stage.at[lane], out, store_sem.at[lane])

    def finish(lane):
        @pl.loop(0, rows // BAND)
        def _(i):
            at = pl.ds(pl.multiple_of(i * BAND, BAND), BAND)
            u, inv = unit_rows(raw[1 - lane, at])
            d = scale * acc[lane, at]
            d = (d - u * jnp.sum(u * d, axis=-1, keepdims=True)) * inv
            stage[lane, at] = d.astype(jnp.bfloat16)

        store(lane).start()

    for w in range(WAVES):
        first_round(w)
        if w == 0:
            prepare()

        @pl.loop(1, HOPS - 1)
        def _(h):
            relay_round(w, h)
            if w == 0 and compute:
                pl.when(h == 2)(own_tile)
            if w > 0:
                @pl.when(h == 1)
                def _():
                    last_pieces(w - 1)

        last_round(w)
        group_pieces(w)

    for lane in (TEXT, IMAGE):
        @pl.loop(0, CHUNKS)
        def _(c):
            chunk = (WAVES - 1) * CHUNKS + c
            arrived(lane, LAST_SLOT, chunk)
            if compute:
                piece(lane, LAST_SLOT, pl.multiple_of(chunk * part, part), part)

        finish(lane)

    for lane in (TEXT, IMAGE):
        for h in range(HOPS):
            pltpu.make_async_remote_copy(
                src_ref=buf.at[lane, 0], dst_ref=buf.at[lane, 0], send_sem=send_sem.at[lane, h],
                recv_sem=recv_sem.at[lane, 0, 0], device_id=following, device_id_type=MESH,
            ).wait_send()
        store(lane).wait()

    def side_done(kind):
        pltpu.make_async_remote_copy(
            src_ref=buf.at[0, 0], dst_ref=buf.at[0, 0], send_sem=side_sem.at[kind],
            recv_sem=recv_sem.at[0, 0, 0], device_id=partner, device_id_type=MESH,
        ).wait_send()

    side_done(0)

    @pl.when(gives)
    def _():
        side_done(1)


COMPUTE = True


def shards(image_emb, text_emb, labels, log_scale, bias):
    rows, width = image_emb.shape
    block = (rows, width)
    whole = pl.BlockSpec(memory_space=pl.ANY)
    vmem = pl.BlockSpec(memory_space=pltpu.VMEM)
    smem = pl.BlockSpec(memory_space=pltpu.SMEM)
    macs = 11 * rows * rows * width
    return pl.pallas_call(
        functools.partial(kernel, rows, COMPUTE),
        name="relay",
        out_shape=[jax.ShapeDtypeStruct(block, jnp.bfloat16)] * 2,
        in_specs=[smem, smem, vmem, whole, whole],
        out_specs=[whole, whole],
        scratch_shapes=[
            pltpu.VMEM((2, *block), jnp.bfloat16),
            pltpu.VMEM((2, *block), jnp.bfloat16),
            pltpu.VMEM((2, *block), jnp.float32),
            pltpu.VMEM((rows // WAVES, width), jnp.bfloat16),
            pltpu.VMEM((2, *block), jnp.bfloat16),
            pltpu.VMEM((2, HOPS + 1, *block), jnp.bfloat16),
            pltpu.SemaphoreType.DMA((2,)),
            pltpu.SemaphoreType.DMA((2, HOPS)),
            pltpu.SemaphoreType.DMA((2, HOPS + 1, WAVES * CHUNKS)),
            pltpu.SemaphoreType.DMA((2,)),
            pltpu.SemaphoreType.DMA((2,)),
        ],
        compiler_params=pltpu.CompilerParams(
            collective_id=0, has_side_effects=True, vmem_limit_bytes=52 * 1024 * 1024
        ),
        cost_estimate=pl.CostEstimate(
            flops=2 * macs, bytes_accessed=8 * rows * width, transcendentals=5 * rows * rows
        ),
    )(log_scale, bias, labels.reshape(1, rows), image_emb, text_emb)


def solution(mesh):
    placed = (P(("group", "blk"), None), P(("group", "blk"), None), P(("group", "blk")), P(), P())
    return jax.shard_map(
        shards,
        mesh=mesh,
        in_specs=placed,
        out_specs=(P(("group", "blk"), None), P(("group", "blk"), None)),
        check_vma=False,
    )
```

```python
import functools

import jax
import jax.numpy as jnp
from jax import lax
from jax.experimental import pallas as pl
from jax.experimental.pallas import tpu as pltpu
from jax.sharding import PartitionSpec as P

EPS = 1e-06
MESH = pl.DeviceIdType.MESH
TEXT, IMAGE = 0, 1
LEGS = (1, 1, 1, 1, 1, 1, 1, 1)
WAVES = 2
CHUNKS = 4
STORE = True
HOPS = len(LEGS)
GROUP_SLOT, LAST_SLOT = HOPS - 1, HOPS
BAND = 128
WIDE = 256
UNIT = 128


def dot_nt(a, b):
    return lax.dot_general(a, b, (((1,), (1,)), ((), ())), preferred_element_type=jnp.float32)


def dot_tn(a, b):
    return lax.dot_general(a, b, (((0,), (0,)), ((), ())), preferred_element_type=jnp.float32)


def unit_rows(v):
    f = v.astype(jnp.float32)
    inv = lax.rsqrt(jnp.sum(f * f, axis=-1, keepdims=True) + EPS)
    return f * inv, inv


def kernel(
    rows, compute, scale_ref, bias_ref, label_ref, image_ref, text_ref, gimage_ref, gtext_ref,
    raw, unit, acc, piece_unit, last_unit, last_q, stage, buf, load_sem, send_sem, recv_sem, side_sem, store_sem,
):
    g, b = lax.axis_index("group"), lax.axis_index("blk")
    core, z_lo = lax.rem(g, 2), lax.div(g, 2)
    z_hi, xy = lax.rem(b, 2), lax.div(b, 2)
    z = z_hi * 8 + z_lo
    other = 1 - core

    def device(z_to, core_to, xy_to):
        z_in = lax.rem(z_to + 32, 16)
        return lax.rem(z_in, 8) * 2 + core_to, lax.rem(xy_to + 16, 16) * 2 + lax.div(z_in, 8)

    def way(c):
        return 2 * c - 1

    def lane_core(lane, z_at, c):
        edge = 7 if lane == TEXT else 0
        return jnp.where(lax.rem(z_at + 32, 8) == edge, 1 - c, c)

    step = way(core)
    middle = sorted(set(LEGS[1:-1]))
    ahead = {leg: device(z + step * leg, core, xy) for leg in middle}
    behind = [device(z - step * leg, core, xy) for leg in middle]
    partner = device(z, other, xy)
    first, first_from, last, last_from = [], [], [], []
    for lane in (TEXT, IMAGE):
        own_lane = lane_core(lane, z, core)
        first.append(device(z + way(own_lane), own_lane, xy))
        first_from.append(device(z - step, lane_core(lane, z - step, core), xy))
        crossing = 0 if lane == TEXT else 1
        shift = 1 if lane == TEXT else -1
        last_hi = lax.div(lax.rem(z + step + 32, 16), 8)
        last.append(
            device(z + step, lane_core(lane, z + step, core), xy + jnp.where(last_hi == crossing, shift, 0))
        )
        last_from.append(
            device(z - way(own_lane), own_lane, xy - jnp.where(z_hi == crossing, shift, 0))
        )

    own = (text_ref, image_ref)
    part = rows // (WAVES * CHUNKS)
    wave_rows = rows // WAVES

    loads = [pltpu.make_async_copy(own[l], raw.at[l], load_sem.at[l]) for l in (TEXT, IMAGE)]
    for load in loads:
        load.start()

    barrier = pltpu.get_barrier_semaphore()
    for source in (*behind, partner, *first_from, *last_from):
        pl.semaphore_signal(barrier, inc=1, device_id=source, device_id_type=MESH)
    pl.semaphore_wait(barrier, 5 + len(behind))

    def chunk_rows(chunk):
        return pl.ds(pl.multiple_of(chunk * part, part), part)

    def hop(lane, src, slot, hop_at, chunk, to):
        at = chunk_rows(chunk)
        return pltpu.make_async_remote_copy(
            src_ref=src.at[at], dst_ref=buf.at[lane, slot, at], send_sem=send_sem.at[lane, hop_at],
            recv_sem=recv_sem.at[lane, slot, chunk], device_id=to, device_id_type=MESH,
        )

    def arrived(lane, slot, chunk):
        hop(lane, buf.at[lane, slot], slot, 0, chunk, partner).wait_recv()

    lane_side = other
    gives = jnp.where(core == 0, z_lo != 7, z_lo != 0)
    takes_lane = jnp.where(core == 0, z_lo == 0, z_lo == 7)

    def side(src, lane, kind, chunk):
        at = chunk_rows(chunk)
        return pltpu.make_async_remote_copy(
            src_ref=src.at[at], dst_ref=buf.at[lane, GROUP_SLOT, at], send_sem=side_sem.at[kind],
            recv_sem=recv_sem.at[lane, GROUP_SLOT, chunk], device_id=partner, device_id_type=MESH,
        )

    lanes = (other, core)

    def pick(lane, pair):
        return tuple(jnp.where(lane == TEXT, t, i) for t, i in zip(*pair))

    def first_round(w):
        for way_core in (0, 1):
            @pl.when(core == way_core)
            def _():
                for lane in (1 - way_core, way_core):
                    @pl.loop(0, CHUNKS)
                    def _(c):
                        hop(lane, own[lane], 0, 0, w * CHUNKS + c, first[lane]).start()

                @pl.loop(0, CHUNKS)
                def _(c):
                    side(own[way_core], way_core, 0, w * CHUNKS + c).start()

    def relay_round(w, h):
        for lane in lanes:
            @pl.loop(0, CHUNKS)
            def _(c):
                chunk = w * CHUNKS + c
                arrived(lane, h - 1, chunk)
                hop(lane, buf.at[lane, h - 1], h, h, chunk, ahead[LEGS[h]]).start()

                if h == 1:
                    @pl.when(gives & (lane_side == lane))
                    def _():
                        side(buf.at[lane, 0], lane, 1, chunk).start()

    def last_round(w):
        for lane in lanes:
            to = pick(lane, last)

            @pl.loop(0, CHUNKS)
            def _(c):
                chunk = w * CHUNKS + c
                arrived(lane, HOPS - 2, chunk)
                hop(lane, buf.at[lane, HOPS - 2], LAST_SLOT, HOPS - 1, chunk, to).start()

    scale = jnp.exp(jnp.full((1, 1), scale_ref[0], jnp.float32))
    shift_b = bias_ref[0]

    def prepare():
        for l in (TEXT, IMAGE):
            loads[l].wait()

            @pl.loop(0, rows // BAND)
            def _(i):
                at = pl.ds(pl.multiple_of(i * BAND, BAND), BAND)
                unit[l, at] = unit_rows(raw[l, at])[0].astype(jnp.bfloat16)

    def own_tile():
        acc[TEXT] = jnp.zeros_like(acc[TEXT])

        @pl.loop(0, rows // BAND)
        def _(i):
            at = pl.ds(pl.multiple_of(i * BAND, BAND), BAND)
            s = scale * dot_nt(unit[TEXT, at], unit[IMAGE]) + shift_b
            text_row = lax.broadcasted_iota(jnp.int32, s.shape, 0) + i * BAND
            label = (text_row == label_ref[...]).astype(jnp.float32)
            q = (jax.nn.sigmoid(s) - label).astype(jnp.bfloat16)
            acc[IMAGE, at] = jnp.dot(q, unit[IMAGE], preferred_element_type=jnp.float32)
            acc[TEXT] += dot_tn(q, unit[TEXT, at])

    def piece(lane, slot, start):
        piece_unit[...] = unit_rows(buf[lane, slot, pl.ds(start, wave_rows)])[0].astype(jnp.bfloat16)

        @pl.loop(0, rows // WIDE)
        def _(i):
            at = pl.ds(pl.multiple_of(i * WIDE, WIDE), WIDE)
            s = scale * dot_nt(unit[1 - lane, at], piece_unit[...]) + shift_b
            q = jax.nn.sigmoid(s).astype(jnp.bfloat16)
            acc[lane, at] += jnp.dot(q, piece_unit[...], preferred_element_type=jnp.float32)

    def group_pieces(w):
        @pl.loop(0, 2)
        def _(lane):
            @pl.when(jnp.logical_not(takes_lane & (core == lane)))
            def _():
                @pl.loop(0, CHUNKS)
                def _(c):
                    arrived(lane, GROUP_SLOT, w * CHUNKS + c)

                if compute:
                    piece(lane, GROUP_SLOT, w * wave_rows)

    def edge_piece(w):
        @pl.when(takes_lane)
        def _():
            if compute:
                piece(core, HOPS - 2, w * wave_rows)

    def last_pieces(w):
        @pl.loop(0, 2)
        def _(n):
            lane = lax.rem(other + n, 2)

            @pl.loop(0, CHUNKS)
            def _(c):
                arrived(lane, LAST_SLOT, w * CHUNKS + c)

            if compute:
                piece(lane, LAST_SLOT, w * wave_rows)

    def weigh(lane, n):
        start = (WAVES - 1) * wave_rows + n * UNIT
        u = unit_rows(buf[lane, LAST_SLOT, pl.ds(start, UNIT)])[0].astype(jnp.bfloat16)
        last_unit[lane, pl.ds(n * UNIT, UNIT)] = u
        s = scale * dot_nt(unit[1 - lane], u) + shift_b
        last_q[lane, :, pl.ds(n * UNIT, UNIT)] = jax.nn.sigmoid(s).astype(jnp.bfloat16)

    def store(lane):
        out = (gimage_ref, gtext_ref)[lane]
        return pltpu.make_async_copy(stage.at[lane], out, store_sem.at[lane])

    def finish(lane):
        @pl.loop(0, rows // BAND)
        def _(i):
            at = pl.ds(pl.multiple_of(i * BAND, BAND), BAND)
            u, inv = unit_rows(raw[1 - lane, at])
            last_part = jnp.dot(last_q[lane, at], last_unit[lane], preferred_element_type=jnp.float32)
            d = scale * (acc[lane, at] + last_part)
            d = (d - u * jnp.sum(u * d, axis=-1, keepdims=True)) * inv
            stage[lane, at] = d.astype(jnp.bfloat16)

        for which in (TEXT, IMAGE):
            @pl.when(lane == which)
            def _():
                store(which).start()

    for w in range(WAVES):
        first_round(w)
        if w == 0:
            prepare()

        for h in range(1, HOPS - 1):
            relay_round(w, h)
            if h == 1:
                if w > 0:
                    last_pieces(w - 1)
                elif compute:
                    own_tile()
            if h == 3:
                group_pieces(w)

        last_round(w)
        edge_piece(w)

    @pl.loop(0, 2)
    def _(n):
        lane = lax.rem(other + n, 2)

        for n in range(wave_rows // UNIT):
            @pl.loop(n * UNIT // part, (n + 1) * UNIT // part)
            def _(c):
                arrived(lane, LAST_SLOT, (WAVES - 1) * CHUNKS + c)

            if compute:
                weigh(lane, n)

        if STORE:
            finish(lane)

    for lane in (TEXT, IMAGE):
        for h in range(HOPS):
            pltpu.make_async_remote_copy(
                src_ref=buf.at[lane, 0], dst_ref=buf.at[lane, 0], send_sem=send_sem.at[lane, h],
                recv_sem=recv_sem.at[lane, 0, 0], device_id=partner, device_id_type=MESH,
            ).wait_send()
        if STORE:
            store(lane).wait()

    def side_done(kind):
        pltpu.make_async_remote_copy(
            src_ref=buf.at[0, 0], dst_ref=buf.at[0, 0], send_sem=side_sem.at[kind],
            recv_sem=recv_sem.at[0, 0, 0], device_id=partner, device_id_type=MESH,
        ).wait_send()

    side_done(0)

    @pl.when(gives)
    def _():
        side_done(1)


COMPUTE = True


def shards(image_emb, text_emb, labels, log_scale, bias):
    rows, width = image_emb.shape
    block = (rows, width)
    whole = pl.BlockSpec(memory_space=pl.ANY)
    vmem = pl.BlockSpec(memory_space=pltpu.VMEM)
    smem = pl.BlockSpec(memory_space=pltpu.SMEM)
    macs = 11 * rows * rows * width
    return pl.pallas_call(
        functools.partial(kernel, rows, COMPUTE),
        name="relay",
        out_shape=[jax.ShapeDtypeStruct(block, jnp.bfloat16)] * 2,
        in_specs=[smem, smem, vmem, whole, whole],
        out_specs=[whole, whole],
        scratch_shapes=[
            pltpu.VMEM((2, *block), jnp.bfloat16),
            pltpu.VMEM((2, *block), jnp.bfloat16),
            pltpu.VMEM((2, *block), jnp.float32),
            pltpu.VMEM((rows // WAVES, width), jnp.bfloat16),
            pltpu.VMEM((2, rows // WAVES, width), jnp.bfloat16),
            pltpu.VMEM((2, rows, rows // WAVES), jnp.bfloat16),
            pltpu.VMEM((2, *block), jnp.bfloat16),
            pltpu.VMEM((2, HOPS + 1, *block), jnp.bfloat16),
            pltpu.SemaphoreType.DMA((2,)),
            pltpu.SemaphoreType.DMA((2, HOPS)),
            pltpu.SemaphoreType.DMA((2, HOPS + 1, WAVES * CHUNKS)),
            pltpu.SemaphoreType.DMA((2,)),
            pltpu.SemaphoreType.DMA((2,)),
        ],
        compiler_params=pltpu.CompilerParams(
            collective_id=0, has_side_effects=True, vmem_limit_bytes=52 * 1024 * 1024
        ),
        cost_estimate=pl.CostEstimate(
            flops=2 * macs, bytes_accessed=8 * rows * width, transcendentals=5 * rows * rows
        ),
    )(log_scale, bias, labels.reshape(1, rows), image_emb, text_emb)


def solution(mesh):
    placed = (P(("group", "blk"), None), P(("group", "blk"), None), P(("group", "blk")), P(), P())
    return jax.shard_map(
        shards,
        mesh=mesh,
        in_specs=placed,
        out_specs=(P(("group", "blk"), None), P(("group", "blk"), None)),
        check_vma=False,
    )
```

```python
import functools

import jax
import jax.numpy as jnp
from jax import lax
from jax.experimental import pallas as pl
from jax.experimental.pallas import tpu as pltpu
from jax.sharding import PartitionSpec as P

EPS = 1e-06
MESH = pl.DeviceIdType.MESH
TEXT, IMAGE = 0, 1
HOPS = 8
TURNS = (3, 1)
WAVES = 2
CHUNKS = 4
GROUP_SLOT, LAST_SLOT, TURN_SLOT = HOPS - 1, HOPS, HOPS + 1
BAND = 128
WIDE = 256
UNIT = 128


def dot_nt(a, b):
    return lax.dot_general(a, b, (((1,), (1,)), ((), ())), preferred_element_type=jnp.float32)


def dot_tn(a, b):
    return lax.dot_general(a, b, (((0,), (0,)), ((), ())), preferred_element_type=jnp.float32)


def unit_rows(v):
    f = v.astype(jnp.float32)
    inv = lax.rsqrt(jnp.sum(f * f, axis=-1, keepdims=True) + EPS)
    return f * inv, inv


def kernel(
    rows, scale_hbm, bias_hbm, label_hbm, image_ref, text_ref, out_ref,
    scale_ref, bias_ref, label_ref, raw, unit, acc, inv_ref, piece_unit, last_unit, last_q, buf, load_sem, send_sem, recv_sem, side_sem, turn_sem,
):
    g, b = lax.axis_index("group"), lax.axis_index("blk")
    core, z_lo = lax.rem(g, 2), lax.div(g, 2)
    xy = lax.div(b, 2)
    z = lax.rem(b, 2) * 8 + z_lo
    other = 1 - core
    step = 2 * core - 1

    def device(z_to, core_to, xy_to):
        z_in = lax.rem(z_to + 32, 16)
        return lax.rem(z_in, 8) * 2 + core_to, lax.rem(xy_to + 16, 16) * 2 + lax.div(z_in, 8)

    def low(z_at):
        return lax.rem(z_at + 32, 8)

    def high(z_at):
        return lax.div(lax.rem(z_at + 32, 16), 8)

    def edge(kind):
        return jnp.where(kind == TEXT, 7, 0)

    def lane_core(kind, z_at, core_at):
        return jnp.where(low(z_at) == edge(kind), 1 - core_at, core_at)

    def swap(lane, z_at, value):
        ends = (low(z_at) == 0) | (low(z_at) == 7)
        return jnp.where((lane == 0) | ends, 1 - value, value)

    def turns(kind, z_source):
        return high(z_source) == jnp.where(kind == TEXT, 1, 0)

    def shift(kind):
        return jnp.where(kind == TEXT, 1, -1)

    partner = device(z, other, xy)
    ahead, behind = device(z + step, core, xy), device(z - step, core, xy)
    columns = (device(z, core, xy - 1), device(z, core, xy + 1))
    first, first_turn, last_from = [], [], []
    for kind in (TEXT, IMAGE):
        lane = lane_core(kind, z, core)
        first.append(device(z + 2 * lane - 1, lane, xy))
        first_turn.append(swap(lane, z, kind))
        last_from.append(device(z - (2 * lane - 1), lane, xy))
    leg = jnp.where(core == 0, *TURNS)
    first_from, turning, turn_to, last, last_kind = [], [], [], [], []
    for n in (0, 1):
        kind = swap(core, z - step, n)
        first_from.append(device(z - step, lane_core(kind, z - step, core), xy))
        kind = swap(core, z - step * leg, n)
        turning.append(turns(kind, z - step * leg))
        turn_to.append(device(z, core, xy + shift(kind)))
        kind = swap(core, z + step, n)
        last_kind.append(kind)
        last.append(device(z + step, lane_core(kind, z + step, core), xy))
    early = jnp.where(first_turn[TEXT] == 0, TEXT, IMAGE)

    own = (text_ref, image_ref)
    part = rows // (WAVES * CHUNKS)
    wave_rows = rows // WAVES

    loads = [pltpu.make_async_copy(own[l], raw.at[l], load_sem.at[l]) for l in (TEXT, IMAGE)]
    small = ((scale_hbm, scale_ref), (bias_hbm, bias_ref), (label_hbm, label_ref))
    loads += [pltpu.make_async_copy(src, dst, load_sem.at[2 + n]) for n, (src, dst) in enumerate(small)]
    for load in loads:
        load.start()

    barrier = pltpu.get_barrier_semaphore()
    for source in (partner, behind, *columns, *first_from, *last_from):
        pl.semaphore_signal(barrier, inc=1, device_id=source, device_id_type=MESH)
    pl.semaphore_wait(barrier, 8)

    def chunk_rows(chunk):
        return pl.ds(pl.multiple_of(chunk * part, part), part)

    def hop(src, at_n, slot, n, leg, chunk, to):
        at = chunk_rows(chunk)
        return pltpu.make_async_remote_copy(
            src_ref=src.at[at], dst_ref=buf.at[at_n, slot, at], send_sem=send_sem.at[n, leg],
            recv_sem=recv_sem.at[at_n, slot, chunk], device_id=to, device_id_type=MESH,
        )

    def send(src, at_n, slot, n, leg, w, c, to):
        hop(src, at_n, slot, n, leg, w * CHUNKS + c, to).start()

    def across(src, at_n, slot, way, chunk, to):
        at = chunk_rows(chunk)
        return pltpu.make_async_remote_copy(
            src_ref=src.at[at], dst_ref=buf.at[at_n, slot, at], send_sem=turn_sem.at[way],
            recv_sem=recv_sem.at[at_n, slot, chunk], device_id=to, device_id_type=MESH,
        )

    def arrived(n, slot, chunk):
        hop(buf.at[n, slot], n, slot, 0, 0, chunk, partner).wait_recv()

    side_kind = other
    side_turn = swap(core, z - step, side_kind)
    gives = jnp.where(core == 0, z_lo != 7, z_lo != 0)
    takes_lane = jnp.where(core == 0, z_lo == 0, z_lo == 7)
    returns = takes_lane & turns(core, z - 7 * step)
    return_to = device(z, core, xy - shift(core))

    def side(src, kind, way, chunk):
        at = chunk_rows(chunk)
        return pltpu.make_async_remote_copy(
            src_ref=src.at[at], dst_ref=buf.at[kind, GROUP_SLOT, at], send_sem=side_sem.at[way],
            recv_sem=recv_sem.at[kind, GROUP_SLOT, chunk], device_id=partner, device_id_type=MESH,
        )

    def first_round(w):
        for kinds in ((TEXT, IMAGE), (IMAGE, TEXT)):
            @pl.when(early == kinds[0])
            def _():
                for kind in kinds:
                    @pl.loop(0, CHUNKS)
                    def _(c):
                        n = first_turn[kind]
                        send(own[kind], n, 0, n, 0, w, c, first[kind])

        for kind in (TEXT, IMAGE):
            @pl.when(core == kind)
            def _():
                @pl.loop(0, CHUNKS)
                def _(c):
                    side(own[kind], kind, 0, w * CHUNKS + c).start()

    def relay_round(w, h):
        def relay(n, slot, to):
            @pl.loop(0, CHUNKS)
            def _(c):
                chunk = w * CHUNKS + c
                arrived(n, slot, chunk)
                send(buf.at[n, slot], n, h, n, h, w, c, to)

                if h == 1 and slot == 0:
                    @pl.when(gives & (side_turn == n))
                    def _():
                        side(buf.at[n, 0], side_kind, 1, chunk).start()

        if h not in TURNS:
            for n in (0, 1):
                relay(n, h - 1, ahead)
            return

        for n in (0, 1):
            turned = turning[n] & (leg == h)

            @pl.when(turned)
            def _():
                @pl.loop(0, CHUNKS)
                def _(c):
                    chunk = w * CHUNKS + c
                    arrived(n, h - 1, chunk)
                    across(buf.at[n, h - 1], n, TURN_SLOT, 0, chunk, turn_to[n]).start()

                    if h == 1:
                        @pl.when(gives & (side_turn == n))
                        def _():
                            side(buf.at[n, 0], side_kind, 1, chunk).start()

            @pl.when(jnp.logical_not(turned))
            def _():
                relay(n, h - 1, ahead)

        for n in (0, 1):
            @pl.when(turning[n] & (leg == h))
            def _():
                relay(n, TURN_SLOT, ahead)

    def last_round(w):
        for n in (0, 1):
            @pl.loop(0, CHUNKS)
            def _(c):
                chunk = w * CHUNKS + c
                arrived(n, HOPS - 2, chunk)
                send(buf.at[n, HOPS - 2], last_kind[n], LAST_SLOT, n, HOPS - 1, w, c, last[n])

                @pl.when(returns & (other == n))
                def _():
                    across(buf.at[n, HOPS - 2], core, GROUP_SLOT, 1, chunk, return_to).start()


    def prepare():
        for l in (TEXT, IMAGE):
            loads[l].wait()

            @pl.loop(0, rows // BAND)
            def _(i):
                at = pl.ds(pl.multiple_of(i * BAND, BAND), BAND)
                u, inv = unit_rows(raw[l, at])
                unit[l, at] = u.astype(jnp.bfloat16)
                inv_ref[l, at] = inv

    def own_tile():
        acc[TEXT] = jnp.zeros_like(acc[TEXT])

        @pl.loop(0, rows // BAND)
        def _(i):
            at = pl.ds(pl.multiple_of(i * BAND, BAND), BAND)
            s = scale * dot_nt(unit[TEXT, at], unit[IMAGE]) + shift_b
            text_row = lax.broadcasted_iota(jnp.int32, s.shape, 0) + i * BAND
            label = (text_row == label_ref[...]).astype(jnp.float32)
            q = (jax.nn.sigmoid(s) - label).astype(jnp.bfloat16)
            acc[IMAGE, at] = jnp.dot(q, unit[IMAGE], preferred_element_type=jnp.float32)
            acc[TEXT] += dot_tn(q, unit[TEXT, at])

    def piece(kind, n, slot, start):
        piece_unit[...] = unit_rows(buf[n, slot, pl.ds(start, wave_rows)])[0].astype(jnp.bfloat16)

        @pl.loop(0, rows // WIDE)
        def _(i):
            at = pl.ds(pl.multiple_of(i * WIDE, WIDE), WIDE)
            s = scale * dot_nt(unit[1 - kind, at], piece_unit[...]) + shift_b
            q = jax.nn.sigmoid(s).astype(jnp.bfloat16)
            acc[kind, at] += jnp.dot(q, piece_unit[...], preferred_element_type=jnp.float32)

    def group_pieces(w):
        @pl.loop(0, 2)
        def _(kind):
            @pl.when(jnp.logical_not(takes_lane & (core == kind)))
            def _():
                @pl.loop(0, CHUNKS)
                def _(c):
                    arrived(kind, GROUP_SLOT, w * CHUNKS + c)

                piece(kind, kind, GROUP_SLOT, w * wave_rows)

    def edge_piece(w):
        @pl.when(takes_lane)
        def _():
            @pl.when(returns)
            def _():
                @pl.loop(0, CHUNKS)
                def _(c):
                    arrived(core, GROUP_SLOT, w * CHUNKS + c)

            at_n, slot = jnp.where(returns, core, other), jnp.where(returns, GROUP_SLOT, HOPS - 2)
            piece(core, at_n, slot, w * wave_rows)

    def last_pieces(w):
        @pl.loop(0, 2)
        def _(n):
            kind = lax.rem(early + n, 2)

            @pl.loop(0, CHUNKS)
            def _(c):
                arrived(kind, LAST_SLOT, w * CHUNKS + c)

            piece(kind, kind, LAST_SLOT, w * wave_rows)

    def weigh(kind, n):
        start = (WAVES - 1) * wave_rows + n * UNIT
        u = unit_rows(buf[kind, LAST_SLOT, pl.ds(start, UNIT)])[0].astype(jnp.bfloat16)
        last_unit[kind, pl.ds(n * UNIT, UNIT)] = u
        s = scale * dot_nt(unit[1 - kind], u) + shift_b
        last_q[kind, :, pl.ds(n * UNIT, UNIT)] = jax.nn.sigmoid(s).astype(jnp.bfloat16)

    def finish(kind):
        @pl.loop(0, rows // BAND)
        def _(i):
            at = pl.ds(pl.multiple_of(i * BAND, BAND), BAND)
            inv = inv_ref[1 - kind, at]
            u = raw[1 - kind, at].astype(jnp.float32) * inv
            last_part = jnp.dot(last_q[kind, at], last_unit[kind], preferred_element_type=jnp.float32)
            d = scale * (acc[kind, at] + last_part)
            d = (d - u * jnp.sum(u * d, axis=-1, keepdims=True)) * inv
            out_ref[kind, at] = d.astype(jnp.bfloat16)

    waves = range(WAVES)
    for w in waves:
        first_round(w)
    for load in loads[2:]:
        load.wait()
    scale = jnp.exp(scale_ref[...])
    shift_b = bias_ref[...]
    prepare()
    for h in range(1, HOPS - 1):
        for w in waves:
            relay_round(w, h)
            if h == 3 + w:
                group_pieces(w)
        if h == 1:
            own_tile()
    for w in waves:
        last_round(w)
        edge_piece(w)
    for w in waves[:-1]:
        last_pieces(w)

    @pl.loop(0, 2)
    def _(n):
        kind = lax.rem(early + n, 2)

        for m in range(wave_rows // UNIT):
            @pl.loop(m * UNIT // part, (m + 1) * UNIT // part)
            def _(c):
                arrived(kind, LAST_SLOT, (WAVES - 1) * CHUNKS + c)

            weigh(kind, m)

        finish(kind)

    def done(sem):
        pltpu.make_async_remote_copy(
            src_ref=buf.at[0, 0], dst_ref=buf.at[0, 0], send_sem=sem,
            recv_sem=recv_sem.at[0, 0, 0], device_id=partner, device_id_type=MESH,
        ).wait_send()

    for n in (0, 1):
        for h in range(HOPS):
            done(send_sem.at[n, h])
    done(side_sem.at[0])
    done(turn_sem.at[0])

    @pl.when(gives)
    def _():
        done(side_sem.at[1])

    @pl.when(returns)
    def _():
        done(turn_sem.at[1])


def place(grads_ref, gimage_ref, gtext_ref, sem):
    copies = [
        pltpu.make_async_copy(grads_ref.at[n], out, sem.at[n]) for n, out in enumerate((gimage_ref, gtext_ref))
    ]
    for copy in copies:
        copy.start()
    for copy in copies:
        copy.wait()


def shards(image_emb, text_emb, labels, log_scale, bias):
    rows, width = image_emb.shape
    block = (rows, width)
    whole = pl.BlockSpec(memory_space=pl.ANY)
    vmem = pl.BlockSpec(memory_space=pltpu.VMEM)
    macs = 11 * rows * rows * width
    grads = pl.pallas_call(
        functools.partial(kernel, rows),
        name="relay",
        out_shape=pltpu.VMEM((2, *block), jnp.bfloat16),
        in_specs=[whole] * 5,
        out_specs=vmem,
        scratch_shapes=[
            pltpu.VMEM((1, 1), jnp.float32),
            pltpu.VMEM((1, 1), jnp.float32),
            pltpu.VMEM((1, rows), jnp.int32),
            pltpu.VMEM((2, *block), jnp.bfloat16),
            pltpu.VMEM((2, *block), jnp.bfloat16),
            pltpu.VMEM((2, *block), jnp.float32),
            pltpu.VMEM((2, rows, 1), jnp.float32),
            pltpu.VMEM((rows // WAVES, width), jnp.bfloat16),
            pltpu.VMEM((2, rows // WAVES, width), jnp.bfloat16),
            pltpu.VMEM((2, rows, rows // WAVES), jnp.bfloat16),
            pltpu.VMEM((2, HOPS + 2, *block), jnp.bfloat16),
            pltpu.SemaphoreType.DMA((5,)),
            pltpu.SemaphoreType.DMA((2, HOPS)),
            pltpu.SemaphoreType.DMA((2, HOPS + 2, WAVES * CHUNKS)),
            pltpu.SemaphoreType.DMA((2,)),
            pltpu.SemaphoreType.DMA((2,)),
        ],
        compiler_params=pltpu.CompilerParams(
            collective_id=0, has_side_effects=True, vmem_limit_bytes=52 * 1024 * 1024
        ),
        cost_estimate=pl.CostEstimate(
            flops=2 * macs, bytes_accessed=8 * rows * width, transcendentals=5 * rows * rows
        ),
    )(log_scale.reshape(1, 1), bias.reshape(1, 1), labels.reshape(1, rows), image_emb, text_emb)
    return pl.pallas_call(
        place,
        name="place",
        out_shape=[jax.ShapeDtypeStruct(block, jnp.bfloat16)] * 2,
        in_specs=[vmem],
        out_specs=[whole, whole],
        scratch_shapes=[pltpu.SemaphoreType.DMA((2,))],
        compiler_params=pltpu.CompilerParams(vmem_limit_bytes=1024 * 1024),
    )(grads)


def solution(mesh):
    placed = (P(("group", "blk"), None), P(("group", "blk"), None), P(("group", "blk")), P(), P())
    return jax.shard_map(
        shards,
        mesh=mesh,
        in_specs=placed,
        out_specs=(P(("group", "blk"), None), P(("group", "blk"), None)),
        check_vma=False,
    )
```

```python
import functools

import jax
import jax.numpy as jnp
from jax import lax
from jax.experimental import pallas as pl
from jax.experimental.pallas import tpu as pltpu
from jax.sharding import PartitionSpec as P

EPS = 1e-06
MESH = pl.DeviceIdType.MESH
TEXT, IMAGE = 0, 1
HOPS = 8
TURNS = (3, 1)
WAVES = 2
CHUNKS = 2
GROUP_SLOT, LAST_SLOT, TURN_SLOT = HOPS - 1, HOPS, HOPS + 1
BAND = 128
WIDE = 256
UNIT = 128


def dot_nt(a, b):
    return lax.dot_general(a, b, (((1,), (1,)), ((), ())), preferred_element_type=jnp.float32)


def dot_tn(a, b):
    return lax.dot_general(a, b, (((0,), (0,)), ((), ())), preferred_element_type=jnp.float32)


def unit_rows(v):
    f = v.astype(jnp.float32)
    inv = lax.rsqrt(jnp.sum(f * f, axis=-1, keepdims=True) + EPS)
    return f * inv, inv


def kernel(
    rows, scale_hbm, bias_hbm, label_hbm, image_ref, text_ref, out_ref,
    scale_ref, bias_ref, label_ref, raw, unit, acc, inv_ref, piece_unit, last_unit, last_q, buf, load_sem, send_sem, recv_sem, side_sem, turn_sem,
):
    g, b = lax.axis_index("group"), lax.axis_index("blk")
    core, z_lo = lax.rem(g, 2), lax.div(g, 2)
    xy = lax.div(b, 2)
    z = lax.rem(b, 2) * 8 + z_lo
    other = 1 - core
    step = 2 * core - 1

    def device(z_to, core_to, xy_to):
        z_in = lax.rem(z_to + 32, 16)
        return lax.rem(z_in, 8) * 2 + core_to, lax.rem(xy_to + 16, 16) * 2 + lax.div(z_in, 8)

    def low(z_at):
        return lax.rem(z_at + 32, 8)

    def high(z_at):
        return lax.div(lax.rem(z_at + 32, 16), 8)

    def edge(kind):
        return jnp.where(kind == TEXT, 7, 0)

    def lane_core(kind, z_at, core_at):
        return jnp.where(low(z_at) == edge(kind), 1 - core_at, core_at)

    def swap(lane, z_at, value):
        return jnp.where((lane == 0) | (low(z_at) == 7), 1 - value, value)

    def turns(kind, z_source):
        return high(z_source) == jnp.where(kind == TEXT, 1, 0)

    def shift(kind):
        return jnp.where(kind == TEXT, 1, -1)

    partner = device(z, other, xy)
    ahead, behind = device(z + step, core, xy), device(z - step, core, xy)
    columns = (device(z, core, xy - 1), device(z, core, xy + 1))
    first, first_turn, last_from = [], [], []
    for kind in (TEXT, IMAGE):
        lane = lane_core(kind, z, core)
        first.append(device(z + 2 * lane - 1, lane, xy))
        first_turn.append(swap(lane, z, kind))
        last_from.append(device(z - (2 * lane - 1), lane, xy))
    leg = jnp.where(core == 0, *TURNS)
    first_from, turning, turn_to, last, last_kind = [], [], [], [], []
    for n in (0, 1):
        kind = swap(core, z - step, n)
        first_from.append(device(z - step, lane_core(kind, z - step, core), xy))
        kind = swap(core, z - step * leg, n)
        turning.append(turns(kind, z - step * leg))
        turn_to.append(device(z, core, xy + shift(kind)))
        kind = swap(core, z + step, n)
        last_kind.append(kind)
        last.append(device(z + step, lane_core(kind, z + step, core), xy))
    early = jnp.where((first_turn[TEXT] == 0) | ((core == 0) & (z == 0)), TEXT, IMAGE)

    own = (text_ref, image_ref)
    part = rows // (WAVES * CHUNKS)
    wave_rows = rows // WAVES

    loads = [pltpu.make_async_copy(own[l], raw.at[l], load_sem.at[l]) for l in (TEXT, IMAGE)]
    small = ((scale_hbm, scale_ref), (bias_hbm, bias_ref), (label_hbm, label_ref))
    loads += [pltpu.make_async_copy(src, dst, load_sem.at[2 + n]) for n, (src, dst) in enumerate(small)]
    for load in loads:
        load.start()

    barrier = pltpu.get_barrier_semaphore()
    for source in (partner, behind, *columns, *first_from, *last_from):
        pl.semaphore_signal(barrier, inc=1, device_id=source, device_id_type=MESH)
    pl.semaphore_wait(barrier, 8)

    def chunk_rows(chunk):
        return pl.ds(pl.multiple_of(chunk * part, part), part)

    def hop(src, at_n, slot, n, leg, chunk, to):
        at = chunk_rows(chunk)
        return pltpu.make_async_remote_copy(
            src_ref=src.at[at], dst_ref=buf.at[at_n, slot, at], send_sem=send_sem.at[n, leg],
            recv_sem=recv_sem.at[at_n, slot, chunk], device_id=to, device_id_type=MESH,
        )

    def send(src, at_n, slot, n, leg, w, c, to):
        hop(src, at_n, slot, n, leg, w * CHUNKS + c, to).start()

    def across(src, at_n, slot, way, chunk, to):
        at = chunk_rows(chunk)
        return pltpu.make_async_remote_copy(
            src_ref=src.at[at], dst_ref=buf.at[at_n, slot, at], send_sem=turn_sem.at[way],
            recv_sem=recv_sem.at[at_n, slot, chunk], device_id=to, device_id_type=MESH,
        )

    def arrived(n, slot, chunk):
        hop(buf.at[n, slot], n, slot, 0, 0, chunk, partner).wait_recv()

    side_kind = other
    side_turn = swap(core, z - step, side_kind)
    gives = jnp.where(core == 0, z_lo != 7, z_lo != 0)
    takes_lane = jnp.where(core == 0, z_lo == 0, z_lo == 7)
    taken_turn = swap(core, z - 7 * step, core)
    returns = takes_lane & turns(core, z - 7 * step)
    return_to = device(z, core, xy - shift(core))

    def side(src, kind, way, chunk):
        at = chunk_rows(chunk)
        return pltpu.make_async_remote_copy(
            src_ref=src.at[at], dst_ref=buf.at[kind, GROUP_SLOT, at], send_sem=side_sem.at[way],
            recv_sem=recv_sem.at[kind, GROUP_SLOT, chunk], device_id=partner, device_id_type=MESH,
        )

    def first_round(w):
        for kinds in ((TEXT, IMAGE), (IMAGE, TEXT)):
            @pl.when(early == kinds[0])
            def _():
                for kind in kinds:
                    @pl.loop(0, CHUNKS)
                    def _(c):
                        n = first_turn[kind]
                        send(own[kind], n, 0, kind, 0, w, c, first[kind])

        for kind in (TEXT, IMAGE):
            @pl.when(core == kind)
            def _():
                @pl.loop(0, CHUNKS)
                def _(c):
                    side(own[kind], kind, 0, w * CHUNKS + c).start()

    def relay_round(w, h):
        def relay(n, slot, to):
            @pl.loop(0, CHUNKS)
            def _(c):
                chunk = w * CHUNKS + c
                arrived(n, slot, chunk)
                send(buf.at[n, slot], n, h, n, h, w, c, to)

                if h == 1 and slot == 0:
                    @pl.when(gives & (side_turn == n))
                    def _():
                        side(buf.at[n, 0], side_kind, 1, chunk).start()

        if h not in TURNS:
            for n in (0, 1):
                relay(n, h - 1, ahead)
            return

        for n in (0, 1):
            turned = turning[n] & (leg == h)

            @pl.when(turned)
            def _():
                @pl.loop(0, CHUNKS)
                def _(c):
                    chunk = w * CHUNKS + c
                    arrived(n, h - 1, chunk)
                    across(buf.at[n, h - 1], n, TURN_SLOT, 0, chunk, turn_to[n]).start()

                    if h == 1:
                        @pl.when(gives & (side_turn == n))
                        def _():
                            side(buf.at[n, 0], side_kind, 1, chunk).start()

            @pl.when(jnp.logical_not(turned))
            def _():
                relay(n, h - 1, ahead)

        for n in (0, 1):
            @pl.when(turning[n] & (leg == h))
            def _():
                relay(n, TURN_SLOT, ahead)

    def last_round(w):
        for n in (0, 1):
            @pl.loop(0, CHUNKS)
            def _(c):
                chunk = w * CHUNKS + c
                arrived(n, HOPS - 2, chunk)
                send(buf.at[n, HOPS - 2], last_kind[n], LAST_SLOT, n, HOPS - 1, w, c, last[n])

                @pl.when(returns & (taken_turn == n))
                def _():
                    across(buf.at[n, HOPS - 2], core, GROUP_SLOT, 1, chunk, return_to).start()


    def prepare():
        for l in (TEXT, IMAGE):
            loads[l].wait()

            @pl.loop(0, rows // BAND)
            def _(i):
                at = pl.ds(pl.multiple_of(i * BAND, BAND), BAND)
                u, inv = unit_rows(raw[l, at])
                unit[l, at] = u.astype(jnp.bfloat16)
                inv_ref[l, at] = inv

    def own_tile():
        acc[TEXT] = jnp.zeros_like(acc[TEXT])

        @pl.loop(0, rows // BAND)
        def _(i):
            at = pl.ds(pl.multiple_of(i * BAND, BAND), BAND)
            s = scale * dot_nt(unit[TEXT, at], unit[IMAGE]) + shift_b
            text_row = lax.broadcasted_iota(jnp.int32, s.shape, 0) + i * BAND
            label = (text_row == label_ref[...]).astype(jnp.float32)
            q = (jax.nn.sigmoid(s) - label).astype(jnp.bfloat16)
            acc[IMAGE, at] = jnp.dot(q, unit[IMAGE], preferred_element_type=jnp.float32)
            acc[TEXT] += dot_tn(q, unit[TEXT, at])

    def piece(kind, n, slot, start):
        piece_unit[...] = unit_rows(buf[n, slot, pl.ds(start, wave_rows)])[0].astype(jnp.bfloat16)

        @pl.loop(0, rows // WIDE)
        def _(i):
            at = pl.ds(pl.multiple_of(i * WIDE, WIDE), WIDE)
            s = scale * dot_nt(unit[1 - kind, at], piece_unit[...]) + shift_b
            q = jax.nn.sigmoid(s).astype(jnp.bfloat16)
            acc[kind, at] += jnp.dot(q, piece_unit[...], preferred_element_type=jnp.float32)

    def group_pieces(w):
        @pl.loop(0, 2)
        def _(kind):
            @pl.when(jnp.logical_not(takes_lane & (core == kind)))
            def _():
                @pl.loop(0, CHUNKS)
                def _(c):
                    arrived(kind, GROUP_SLOT, w * CHUNKS + c)

                piece(kind, kind, GROUP_SLOT, w * wave_rows)

    def edge_piece(w):
        @pl.when(takes_lane)
        def _():
            @pl.when(returns)
            def _():
                @pl.loop(0, CHUNKS)
                def _(c):
                    arrived(core, GROUP_SLOT, w * CHUNKS + c)

            at_n, slot = jnp.where(returns, core, taken_turn), jnp.where(returns, GROUP_SLOT, HOPS - 2)
            piece(core, at_n, slot, w * wave_rows)

    def last_pieces(w):
        @pl.loop(0, 2)
        def _(n):
            kind = lax.rem(early + n, 2)

            @pl.loop(0, CHUNKS)
            def _(c):
                arrived(kind, LAST_SLOT, w * CHUNKS + c)

            piece(kind, kind, LAST_SLOT, w * wave_rows)

    def weigh(kind, n):
        start = (WAVES - 1) * wave_rows + n * UNIT
        u = unit_rows(buf[kind, LAST_SLOT, pl.ds(start, UNIT)])[0].astype(jnp.bfloat16)
        last_unit[kind, pl.ds(n * UNIT, UNIT)] = u
        s = scale * dot_nt(unit[1 - kind], u) + shift_b
        last_q[kind, :, pl.ds(n * UNIT, UNIT)] = jax.nn.sigmoid(s).astype(jnp.bfloat16)

    def finish(kind):
        @pl.loop(0, rows // BAND)
        def _(i):
            at = pl.ds(pl.multiple_of(i * BAND, BAND), BAND)
            inv = inv_ref[1 - kind, at]
            u = raw[1 - kind, at].astype(jnp.float32) * inv
            last_part = jnp.dot(last_q[kind, at], last_unit[kind], preferred_element_type=jnp.float32)
            d = scale * (acc[kind, at] + last_part)
            d = (d - u * jnp.sum(u * d, axis=-1, keepdims=True)) * inv
            out_ref[kind, at] = d.astype(jnp.bfloat16)

    waves = range(WAVES)
    for w in waves:
        first_round(w)
    for load in loads[2:]:
        load.wait()
    scale = jnp.exp(scale_ref[...])
    shift_b = bias_ref[...]
    prepare()
    for h in range(1, HOPS - 1):
        for w in waves:
            relay_round(w, h)
            if h == 3 + w:
                group_pieces(w)
        if h == 1:
            own_tile()
    for w in waves:
        last_round(w)
        edge_piece(w)
    for w in waves[:-1]:
        last_pieces(w)

    @pl.loop(0, 2)
    def _(n):
        kind = lax.rem(early + n, 2)

        for m in range(wave_rows // UNIT):
            @pl.loop(m * UNIT // part, (m + 1) * UNIT // part)
            def _(c):
                arrived(kind, LAST_SLOT, (WAVES - 1) * CHUNKS + c)

            weigh(kind, m)

        finish(kind)

    def done(sem):
        pltpu.make_async_remote_copy(
            src_ref=buf.at[0, 0], dst_ref=buf.at[0, 0], send_sem=sem,
            recv_sem=recv_sem.at[0, 0, 0], device_id=partner, device_id_type=MESH,
        ).wait_send()

    for n in (0, 1):
        for h in range(HOPS):
            done(send_sem.at[n, h])
    done(side_sem.at[0])
    done(turn_sem.at[0])

    @pl.when(gives)
    def _():
        done(side_sem.at[1])

    @pl.when(returns)
    def _():
        done(turn_sem.at[1])


def place(grads_ref, gimage_ref, gtext_ref, sem):
    copies = [
        pltpu.make_async_copy(grads_ref.at[n], out, sem.at[n]) for n, out in enumerate((gimage_ref, gtext_ref))
    ]
    for copy in copies:
        copy.start()
    for copy in copies:
        copy.wait()


def shards(image_emb, text_emb, labels, log_scale, bias):
    rows, width = image_emb.shape
    block = (rows, width)
    whole = pl.BlockSpec(memory_space=pl.ANY)
    vmem = pl.BlockSpec(memory_space=pltpu.VMEM)
    macs = 11 * rows * rows * width
    grads = pl.pallas_call(
        functools.partial(kernel, rows),
        name="relay",
        out_shape=pltpu.VMEM((2, *block), jnp.bfloat16),
        in_specs=[whole] * 5,
        out_specs=vmem,
        scratch_shapes=[
            pltpu.VMEM((1, 1), jnp.float32),
            pltpu.VMEM((1, 1), jnp.float32),
            pltpu.VMEM((1, rows), jnp.int32),
            pltpu.VMEM((2, *block), jnp.bfloat16),
            pltpu.VMEM((2, *block), jnp.bfloat16),
            pltpu.VMEM((2, *block), jnp.float32),
            pltpu.VMEM((2, rows, 1), jnp.float32),
            pltpu.VMEM((rows // WAVES, width), jnp.bfloat16),
            pltpu.VMEM((2, rows // WAVES, width), jnp.bfloat16),
            pltpu.VMEM((2, rows, rows // WAVES), jnp.bfloat16),
            pltpu.VMEM((2, HOPS + 2, *block), jnp.bfloat16),
            pltpu.SemaphoreType.DMA((5,)),
            pltpu.SemaphoreType.DMA((2, HOPS)),
            pltpu.SemaphoreType.DMA((2, HOPS + 2, WAVES * CHUNKS)),
            pltpu.SemaphoreType.DMA((2,)),
            pltpu.SemaphoreType.DMA((2,)),
        ],
        compiler_params=pltpu.CompilerParams(
            collective_id=0, has_side_effects=True, vmem_limit_bytes=52 * 1024 * 1024
        ),
        cost_estimate=pl.CostEstimate(
            flops=2 * macs, bytes_accessed=8 * rows * width, transcendentals=5 * rows * rows
        ),
    )(log_scale.reshape(1, 1), bias.reshape(1, 1), labels.reshape(1, rows), image_emb, text_emb)
    return pl.pallas_call(
        place,
        name="place",
        out_shape=[jax.ShapeDtypeStruct(block, jnp.bfloat16)] * 2,
        in_specs=[vmem],
        out_specs=[whole, whole],
        scratch_shapes=[pltpu.SemaphoreType.DMA((2,))],
        compiler_params=pltpu.CompilerParams(vmem_limit_bytes=1024 * 1024),
    )(grads)


def solution(mesh):
    placed = (P(("group", "blk"), None), P(("group", "blk"), None), P(("group", "blk")), P(), P())
    return jax.shard_map(
        shards,
        mesh=mesh,
        in_specs=placed,
        out_specs=(P(("group", "blk"), None), P(("group", "blk"), None)),
        check_vma=False,
    )
```

```python
import functools

import jax
import jax.numpy as jnp
from jax import lax
from jax.experimental import pallas as pl
from jax.experimental.pallas import tpu as pltpu
from jax.sharding import PartitionSpec as P

EPS = 1e-06
MESH = pl.DeviceIdType.MESH
TEXT, IMAGE = 0, 1
HOPS = 8
TURNS = (3, 1)
WAVES = 2
CHUNKS = 2
PARTS = 4
GROUP_SLOT, LAST_SLOT, TURN_SLOT = HOPS - 1, HOPS, HOPS + 1
BAND = 128
WIDE = 256
UNIT = 128


def dot_nt(a, b):
    return lax.dot_general(a, b, (((1,), (1,)), ((), ())), preferred_element_type=jnp.float32)


def dot_tn(a, b):
    return lax.dot_general(a, b, (((0,), (0,)), ((), ())), preferred_element_type=jnp.float32)


def unit_rows(v):
    f = v.astype(jnp.float32)
    inv = lax.rsqrt(jnp.sum(f * f, axis=-1, keepdims=True) + EPS)
    return f * inv, inv


def kernel(
    rows, scale_hbm, bias_hbm, label_hbm, image_ref, text_ref, out_ref,
    scale_ref, bias_ref, label_ref, raw, unit, acc, inv_ref, piece_unit, last_unit, last_q, buf, load_sem, send_sem, recv_sem, side_sem, turn_sem,
):
    g, b = lax.axis_index("group"), lax.axis_index("blk")
    core, z_lo = lax.rem(g, 2), lax.div(g, 2)
    xy = lax.div(b, 2)
    z = lax.rem(b, 2) * 8 + z_lo
    other = 1 - core
    step = 2 * core - 1

    def device(z_to, core_to, xy_to):
        z_in = lax.rem(z_to + 32, 16)
        return lax.rem(z_in, 8) * 2 + core_to, lax.rem(xy_to + 16, 16) * 2 + lax.div(z_in, 8)

    def low(z_at):
        return lax.rem(z_at + 32, 8)

    def high(z_at):
        return lax.div(lax.rem(z_at + 32, 16), 8)

    def edge(kind):
        return jnp.where(kind == TEXT, 7, 0)

    def lane_core(kind, z_at, core_at):
        return jnp.where(low(z_at) == edge(kind), 1 - core_at, core_at)

    def swap(lane, z_at, value):
        return jnp.where((lane == 0) | (low(z_at) == 7), 1 - value, value)

    def turns(kind, z_source):
        return high(z_source) == jnp.where(kind == TEXT, 1, 0)

    def shift(kind):
        return jnp.where(kind == TEXT, 1, -1)

    partner = device(z, other, xy)
    ahead, behind = device(z + step, core, xy), device(z - step, core, xy)
    columns = (device(z, core, xy - 1), device(z, core, xy + 1))
    first, first_turn, last_from = [], [], []
    for kind in (TEXT, IMAGE):
        lane = lane_core(kind, z, core)
        first.append(device(z + 2 * lane - 1, lane, xy))
        first_turn.append(swap(lane, z, kind))
        last_from.append(device(z - (2 * lane - 1), lane, xy))
    leg = jnp.where(core == 0, *TURNS)
    first_from, turning, turn_to, last, last_kind = [], [], [], [], []
    for n in (0, 1):
        kind = swap(core, z - step, n)
        first_from.append(device(z - step, lane_core(kind, z - step, core), xy))
        kind = swap(core, z - step * leg, n)
        turning.append(turns(kind, z - step * leg))
        turn_to.append(device(z, core, xy + shift(kind)))
        kind = swap(core, z + step, n)
        last_kind.append(kind)
        last.append(device(z + step, lane_core(kind, z + step, core), xy))
    early = jnp.where((first_turn[TEXT] == 0) | ((core == 0) & (z == 0)), TEXT, IMAGE)

    own = (text_ref, image_ref)
    part = rows // (WAVES * CHUNKS)
    wave_rows = rows // WAVES

    loads = [pltpu.make_async_copy(own[l], raw.at[l], load_sem.at[l]) for l in (TEXT, IMAGE)]
    small = ((scale_hbm, scale_ref), (bias_hbm, bias_ref), (label_hbm, label_ref))
    loads += [pltpu.make_async_copy(src, dst, load_sem.at[2 + n]) for n, (src, dst) in enumerate(small)]
    for load in loads:
        load.start()

    barrier = pltpu.get_barrier_semaphore()
    for source in (partner, behind, *columns, *first_from, *last_from):
        pl.semaphore_signal(barrier, inc=1, device_id=source, device_id_type=MESH)
    pl.semaphore_wait(barrier, 8)

    def chunk_rows(chunk):
        return pl.ds(pl.multiple_of(chunk * part, part), part)

    def hop(src, at_n, slot, n, leg, chunk, to):
        at = chunk_rows(chunk)
        return pltpu.make_async_remote_copy(
            src_ref=src.at[at], dst_ref=buf.at[at_n, slot, at], send_sem=send_sem.at[n, leg],
            recv_sem=recv_sem.at[at_n, slot, chunk], device_id=to, device_id_type=MESH,
        )

    def send(src, at_n, slot, n, leg, w, c, to):
        hop(src, at_n, slot, n, leg, w * CHUNKS + c, to).start()

    def across(src, at_n, slot, way, chunk, to):
        at = chunk_rows(chunk)
        return pltpu.make_async_remote_copy(
            src_ref=src.at[at], dst_ref=buf.at[at_n, slot, at], send_sem=turn_sem.at[way],
            recv_sem=recv_sem.at[at_n, slot, chunk], device_id=to, device_id_type=MESH,
        )

    def arrived(n, slot, chunk):
        hop(buf.at[n, slot], n, slot, 0, 0, chunk, partner).wait_recv()

    side_kind = other
    side_turn = swap(core, z - step, side_kind)
    gives = jnp.where(core == 0, z_lo != 7, z_lo != 0)
    takes_lane = jnp.where(core == 0, z_lo == 0, z_lo == 7)
    taken_turn = swap(core, z - 7 * step, core)
    returns = takes_lane & turns(core, z - 7 * step)
    return_to = device(z, core, xy - shift(core))

    def side(src, kind, way, chunk):
        at = chunk_rows(chunk)
        return pltpu.make_async_remote_copy(
            src_ref=src.at[at], dst_ref=buf.at[kind, GROUP_SLOT, at], send_sem=side_sem.at[way],
            recv_sem=recv_sem.at[kind, GROUP_SLOT, chunk], device_id=partner, device_id_type=MESH,
        )

    def first_round(w):
        for kinds in ((TEXT, IMAGE), (IMAGE, TEXT)):
            @pl.when(early == kinds[0])
            def _():
                for kind in kinds:
                    @pl.loop(0, CHUNKS)
                    def _(c):
                        n = first_turn[kind]
                        send(own[kind], n, 0, kind, 0, w, c, first[kind])

        for kind in (TEXT, IMAGE):
            @pl.when(core == kind)
            def _():
                @pl.loop(0, CHUNKS)
                def _(c):
                    side(own[kind], kind, 0, w * CHUNKS + c).start()

    def relay_round(w, h):
        def relay(n, slot, to):
            @pl.loop(0, CHUNKS)
            def _(c):
                chunk = w * CHUNKS + c
                arrived(n, slot, chunk)
                send(buf.at[n, slot], n, h, n, h, w, c, to)

                if h == 1 and slot == 0:
                    @pl.when(gives & (side_turn == n))
                    def _():
                        side(buf.at[n, 0], side_kind, 1, chunk).start()

        if h not in TURNS:
            for n in (0, 1):
                relay(n, h - 1, ahead)
            return

        for n in (0, 1):
            turned = turning[n] & (leg == h)

            @pl.when(turned)
            def _():
                @pl.loop(0, CHUNKS)
                def _(c):
                    chunk = w * CHUNKS + c
                    arrived(n, h - 1, chunk)
                    across(buf.at[n, h - 1], n, TURN_SLOT, 0, chunk, turn_to[n]).start()

                    if h == 1:
                        @pl.when(gives & (side_turn == n))
                        def _():
                            side(buf.at[n, 0], side_kind, 1, chunk).start()

            @pl.when(jnp.logical_not(turned))
            def _():
                relay(n, h - 1, ahead)

        for n in (0, 1):
            @pl.when(turning[n] & (leg == h))
            def _():
                relay(n, TURN_SLOT, ahead)

    def last_round(w):
        for n in (0, 1):
            @pl.loop(0, CHUNKS)
            def _(c):
                chunk = w * CHUNKS + c
                arrived(n, HOPS - 2, chunk)
                send(buf.at[n, HOPS - 2], last_kind[n], LAST_SLOT, n, HOPS - 1, w, c, last[n])

                @pl.when(returns & (taken_turn == n))
                def _():
                    across(buf.at[n, HOPS - 2], core, GROUP_SLOT, 1, chunk, return_to).start()


    def prepare():
        for l in (TEXT, IMAGE):
            loads[l].wait()

            @pl.loop(0, rows // BAND)
            def _(i):
                at = pl.ds(pl.multiple_of(i * BAND, BAND), BAND)
                u, inv = unit_rows(raw[l, at])
                unit[l, at] = u.astype(jnp.bfloat16)
                inv_ref[l, at] = inv

    def own_tile():
        acc[TEXT] = jnp.zeros_like(acc[TEXT])

        @pl.loop(0, rows // BAND)
        def _(i):
            at = pl.ds(pl.multiple_of(i * BAND, BAND), BAND)
            s = scale * dot_nt(unit[TEXT, at], unit[IMAGE]) + shift_b
            text_row = lax.broadcasted_iota(jnp.int32, s.shape, 0) + i * BAND
            label = (text_row == label_ref[...]).astype(jnp.float32)
            q = (jax.nn.sigmoid(s) - label).astype(jnp.bfloat16)
            acc[IMAGE, at] = jnp.dot(q, unit[IMAGE], preferred_element_type=jnp.float32)
            acc[TEXT] += dot_tn(q, unit[TEXT, at])

    def piece(kind, n, slot, start):
        piece_unit[...] = unit_rows(buf[n, slot, pl.ds(start, wave_rows)])[0].astype(jnp.bfloat16)

        @pl.loop(0, rows // WIDE)
        def _(i):
            at = pl.ds(pl.multiple_of(i * WIDE, WIDE), WIDE)
            s = scale * dot_nt(unit[1 - kind, at], piece_unit[...]) + shift_b
            q = jax.nn.sigmoid(s).astype(jnp.bfloat16)
            acc[kind, at] += jnp.dot(q, piece_unit[...], preferred_element_type=jnp.float32)

    def group_pieces(w):
        @pl.loop(0, 2)
        def _(kind):
            @pl.when(jnp.logical_not(takes_lane & (core == kind)))
            def _():
                @pl.loop(0, CHUNKS)
                def _(c):
                    arrived(kind, GROUP_SLOT, w * CHUNKS + c)

                piece(kind, kind, GROUP_SLOT, w * wave_rows)

    def edge_piece(w):
        @pl.when(takes_lane)
        def _():
            @pl.when(returns)
            def _():
                @pl.loop(0, CHUNKS)
                def _(c):
                    arrived(core, GROUP_SLOT, w * CHUNKS + c)

            at_n, slot = jnp.where(returns, core, taken_turn), jnp.where(returns, GROUP_SLOT, HOPS - 2)
            piece(core, at_n, slot, w * wave_rows)

    def last_pieces(w):
        @pl.loop(0, 2)
        def _(n):
            kind = lax.rem(early + n, 2)

            @pl.loop(0, CHUNKS)
            def _(c):
                arrived(kind, LAST_SLOT, w * CHUNKS + c)

            piece(kind, kind, LAST_SLOT, w * wave_rows)

    def weigh(kind, n):
        start = (WAVES - 1) * wave_rows + n * UNIT
        u = unit_rows(buf[kind, LAST_SLOT, pl.ds(start, UNIT)])[0].astype(jnp.bfloat16)
        last_unit[kind, pl.ds(n * UNIT, UNIT)] = u
        s = scale * dot_nt(unit[1 - kind], u) + shift_b
        last_q[kind, :, pl.ds(n * UNIT, UNIT)] = jax.nn.sigmoid(s).astype(jnp.bfloat16)

    def finish(kind):
        @pl.loop(0, rows // BAND)
        def _(i):
            at = pl.ds(pl.multiple_of(i * BAND, BAND), BAND)
            inv = inv_ref[1 - kind, at]
            u = raw[1 - kind, at].astype(jnp.float32) * inv
            last_part = jnp.dot(last_q[kind, at], last_unit[kind], preferred_element_type=jnp.float32)
            d = scale * (acc[kind, at] + last_part)
            d = (d - u * jnp.sum(u * d, axis=-1, keepdims=True)) * inv
            out_ref[kind, at] = d.astype(jnp.bfloat16)

    waves = range(WAVES)
    for w in waves:
        first_round(w)
    for load in loads[2:]:
        load.wait()
    scale = jnp.exp(scale_ref[...])
    shift_b = bias_ref[...]
    prepare()
    for h in range(1, HOPS - 1):
        for w in waves:
            relay_round(w, h)
            if h == 3 + w:
                group_pieces(w)
        if h == 1:
            own_tile()
    for w in waves:
        last_round(w)
        edge_piece(w)
    for w in waves[:-1]:
        last_pieces(w)

    @pl.loop(0, 2)
    def _(n):
        kind = lax.rem(early + n, 2)

        for m in range(wave_rows // UNIT):
            @pl.loop(m * UNIT // part, (m + 1) * UNIT // part)
            def _(c):
                arrived(kind, LAST_SLOT, (WAVES - 1) * CHUNKS + c)

            weigh(kind, m)

        finish(kind)

    def done(sem):
        pltpu.make_async_remote_copy(
            src_ref=buf.at[0, 0], dst_ref=buf.at[0, 0], send_sem=sem,
            recv_sem=recv_sem.at[0, 0, 0], device_id=partner, device_id_type=MESH,
        ).wait_send()

    for n in (0, 1):
        for h in range(HOPS):
            done(send_sem.at[n, h])
    done(side_sem.at[0])
    done(turn_sem.at[0])

    @pl.when(gives)
    def _():
        done(side_sem.at[1])

    @pl.when(returns)
    def _():
        done(turn_sem.at[1])


def place(grads_ref, gimage_ref, gtext_ref, sem):
    part = gimage_ref.shape[0] // PARTS
    copies = []
    for n, out in enumerate((gimage_ref, gtext_ref)):
        for m in range(PARTS):
            at = pl.ds(m * part, part)
            copies.append(pltpu.make_async_copy(grads_ref.at[n, at], out.at[at], sem.at[n, m]))
    for copy in copies:
        copy.start()
    for copy in copies:
        copy.wait()


def shards(image_emb, text_emb, labels, log_scale, bias):
    rows, width = image_emb.shape
    block = (rows, width)
    whole = pl.BlockSpec(memory_space=pl.ANY)
    vmem = pl.BlockSpec(memory_space=pltpu.VMEM)
    macs = 11 * rows * rows * width
    grads = pl.pallas_call(
        functools.partial(kernel, rows),
        name="relay",
        out_shape=pltpu.VMEM((2, *block), jnp.bfloat16),
        in_specs=[whole] * 5,
        out_specs=vmem,
        scratch_shapes=[
            pltpu.VMEM((1, 1), jnp.float32),
            pltpu.VMEM((1, 1), jnp.float32),
            pltpu.VMEM((1, rows), jnp.int32),
            pltpu.VMEM((2, *block), jnp.bfloat16),
            pltpu.VMEM((2, *block), jnp.bfloat16),
            pltpu.VMEM((2, *block), jnp.float32),
            pltpu.VMEM((2, rows, 1), jnp.float32),
            pltpu.VMEM((rows // WAVES, width), jnp.bfloat16),
            pltpu.VMEM((2, rows // WAVES, width), jnp.bfloat16),
            pltpu.VMEM((2, rows, rows // WAVES), jnp.bfloat16),
            pltpu.VMEM((2, HOPS + 2, *block), jnp.bfloat16),
            pltpu.SemaphoreType.DMA((5,)),
            pltpu.SemaphoreType.DMA((2, HOPS)),
            pltpu.SemaphoreType.DMA((2, HOPS + 2, WAVES * CHUNKS)),
            pltpu.SemaphoreType.DMA((2,)),
            pltpu.SemaphoreType.DMA((2,)),
        ],
        compiler_params=pltpu.CompilerParams(
            collective_id=0, has_side_effects=True, vmem_limit_bytes=52 * 1024 * 1024
        ),
        cost_estimate=pl.CostEstimate(
            flops=2 * macs, bytes_accessed=8 * rows * width, transcendentals=5 * rows * rows
        ),
    )(log_scale.reshape(1, 1), bias.reshape(1, 1), labels.reshape(1, rows), image_emb, text_emb)
    return pl.pallas_call(
        place,
        name="place",
        out_shape=[jax.ShapeDtypeStruct(block, jnp.bfloat16)] * 2,
        in_specs=[vmem],
        out_specs=[whole, whole],
        scratch_shapes=[pltpu.SemaphoreType.DMA((2, PARTS))],
        compiler_params=pltpu.CompilerParams(vmem_limit_bytes=1024 * 1024),
    )(grads)


def solution(mesh):
    placed = (P(("group", "blk"), None), P(("group", "blk"), None), P(("group", "blk")), P(), P())
    return jax.shard_map(
        shards,
        mesh=mesh,
        in_specs=placed,
        out_specs=(P(("group", "blk"), None), P(("group", "blk"), None)),
        check_vma=False,
    )
```
